32 devices in a mesh: dp: 4 (over y, x), tensor: 8 (over z, core).
Axes of the slice: x: 2, y: 2, z: 4, core: 2. Of those that a mesh axis runs over, the one named last changes fastest.
Arguments:
- hidden: bfloat16 [3072, 20480], P('dp', 'tensor'), may hold values from -6 to 6
- out_grad: bfloat16 [3072, 8192], P('dp', 'tensor'), may hold values from -6 to 6
- w_down: bfloat16 [20480, 8192], P('tensor'), may hold values from -0.0625 to 0.0625
- proj_in: bfloat16 [64, 20480], P(None, 'tensor'), may hold values from -0.0390625 to 0.0390625
- proj_out: bfloat16 [64, 8192], P(None, 'tensor'), may hold values from -0.0625 to 0.0625
- queries: bfloat16 [1024, 4096], P('tensor'), may hold values from -0.005859375 to 0.005859375
- assignment: int32 [12], replicated, may hold values from 0 to 7
Outputs:
- input_grad: bfloat16 [3072, 20480], P('dp', 'tensor')
- scores: float32 [8, 1024], P('dp', 'tensor')
The draws below stay inside these ranges and needn't reach their ends.
All inputs are finite; a program needn't handle non-finite values.
Results may differ from the reference program's by a relative error of at most 0.001.
Values may be sent and summed in bfloat16 or wider, within the bound.
A program may use at most 128 MiB of HBM per device.

```python
import jax
import jax.numpy as jnp
from jax import lax

D = 8192
FF = 20480
K = 64
LEN = 256
Q = 1024
SEQS = 12
TOKENS = 3072
EXAMPLES = 8


def with_ends(array, key, low, high):
    extent = array.shape
    place = [jax.random.randint(jax.random.fold_in(key, axis), (), 0, extent[axis]) for axis in range(len(extent))]
    array = array.at[tuple(place)].set(low)
    longest = extent.index(max(extent))
    place[longest] = (place[longest] + 1) % extent[longest]
    return array.at[tuple(place)].set(high)


def steps_of(own_key, dims, shards, least, high):
    gain = 1.0
    for position, blocks in shards:
        heights = jax.random.uniform(jax.random.fold_in(jax.random.fold_in(own_key, 6), position), (blocks,), jnp.float32, least / len(shards), high / len(shards))
        gain = gain * jnp.repeat(jnp.exp(heights), dims[position] // blocks).reshape((-1,) + (1,) * (len(dims) - 1 - position))
    return gain


def gaussian(stream_key, shape, spread, most, shards=(), kind=jnp.bfloat16):
    drawn = jax.random.normal(stream_key, shape, jnp.float32) * spread
    if len(shards) > 0:
        drawn = steps_of(stream_key, shape, shards, -0.22, 0.18) * drawn
    return jnp.clip(drawn, min=-most, max=most).astype(kind)


def setup_inputs(seed: int = 0) -> dict:
    keys = jax.random.split(jax.random.key(seed), 8)
    return {
        "hidden": gaussian(keys[0], (TOKENS, FF), 1.0, 6.0, ((0, 4), (1, 8))),
        "out_grad": gaussian(keys[1], (TOKENS, D), 1.0, 6.0, ((0, 4), (1, 8))),
        "w_down": gaussian(keys[2], (FF, D), D ** -0.5, 0.0625, ((0, 8),)),
        "proj_in": gaussian(keys[3], (K, FF), FF ** -0.5, 0.0390625, ((1, 8),)),
        "proj_out": gaussian(keys[4], (K, D), D ** -0.5, 0.0625, ((1, 8),)),
        "queries": gaussian(keys[5], (Q, K * K), (K * K * LEN) ** -0.5, 0.005859375, ((0, 8),)),
        "assignment": with_ends(jax.random.randint(keys[6], (SEQS,), 0, EXAMPLES), jax.random.fold_in(keys[6], 1), 0, EXAMPLES - 1).astype(jnp.int32),
    }


def reference(hidden, out_grad, w_down, proj_in, proj_out, queries, assignment):
    input_grad = jnp.dot(out_grad, w_down.T, preferred_element_type=jnp.float32).astype(jnp.bfloat16)
    act_low = jnp.dot(hidden, proj_in.T, preferred_element_type=jnp.float32)
    grad_low = jnp.dot(out_grad, proj_out.T, preferred_element_type=jnp.float32)
    act_seq = act_low.reshape(SEQS, LEN, K)
    grad_seq = grad_low.reshape(SEQS, LEN, K)
    seq_grads = jnp.einsum("slk,slm->skm", act_seq, grad_seq, precision=lax.Precision.HIGHEST).reshape(SEQS, K * K)
    one_hot = (assignment[:, None] == jnp.arange(EXAMPLES, dtype=jnp.int32)[None, :]).astype(jnp.float32)
    example_grads = jnp.dot(one_hot.T, seq_grads, precision=lax.Precision.HIGHEST)
    scores = jnp.dot(example_grads, queries.astype(jnp.float32).T, precision=lax.Precision.HIGHEST)
    return input_grad, scores
```

```python
import jax
import jax.numpy as jnp
from jax import lax
from jax.sharding import PartitionSpec as P

LEN = 256
EX_DEV = 2


def on_device(hidden, out_grad, w_down, proj_in, proj_out, queries, assignment):
    tok_rows = hidden.shape[0]
    seq_count = tok_rows // LEN
    act_part = jnp.einsum("tf,kf->tk", hidden, proj_in, preferred_element_type=jnp.float32)
    grad_part = jnp.einsum("td,kd->tk", out_grad, proj_out, preferred_element_type=jnp.float32)
    low = lax.psum(jnp.concatenate([act_part, grad_part], axis=1), "tensor")
    act_low, second = jnp.split(low, 2, axis=1)
    blocks = []
    for start in range(0, tok_rows, LEN):
        piece = lax.all_gather(out_grad[start:start + LEN], "tensor", axis=1, tiled=True)
        first = jnp.einsum("td,fd->tf", piece, w_down, preferred_element_type=jnp.float32)
        blocks.append(first.astype(jnp.bfloat16))
    input_grad = jnp.concatenate(blocks, axis=0)
    width = act_low.shape[1]
    act_seq = act_low.reshape(seq_count, LEN, width)
    grad_seq = second.reshape(seq_count, LEN, width)
    proj_grads = jnp.einsum(
        "slk,slm->skm", act_seq, grad_seq, precision=lax.Precision.HIGHEST
    ).reshape(seq_count, width * width)
    query_wide = queries.astype(jnp.float32)
    all_grads = lax.all_gather(proj_grads, "dp", axis=0, tiled=True)
    first_example = lax.axis_index("dp") * EX_DEV
    example_ids = first_example + jnp.arange(EX_DEV, dtype=jnp.int32)
    one_hot = (example_ids[:, None] == assignment[None, :]).astype(jnp.float32)
    example_grads = jnp.dot(one_hot, all_grads, precision=lax.Precision.HIGHEST)
    scores = jnp.dot(example_grads, query_wide.T, precision=lax.Precision.HIGHEST)
    return (input_grad, scores)


def solution(mesh):
    placed = (
        P("dp", "tensor"),
        P("dp", "tensor"),
        P("tensor", None),
        P(None, "tensor"),
        P(None, "tensor"),
        P("tensor", None),
        P(),
    )
    return jax.shard_map(
        on_device,
        mesh=mesh,
        in_specs=placed,
        out_specs=(P("dp", "tensor"), P("dp", "tensor")),
        check_vma=False,
    )
```
